32 devices in a mesh: row: 8 (over y, x, core), col: 4 (over z).
Axes of the slice: x: 2, y: 2, z: 4, core: 2. Of those that a mesh axis runs over, the one named last changes fastest.
Arguments:
- hamiltonian: float32 [512, 512], P('row', 'col'), as said below
- tile_mask: int32 [2, 2], replicated, may hold values from 0 to 1, as said below
- start_block: float32 [512, 32], P(('row', 'col')), may hold values from -6 to 6
Outputs:
- states: float32 [512, 32], P(('row', 'col'))
- ritz_matrix: float32 [32, 32], replicated
The draws below stay inside these ranges and needn't reach their ends.
Inputs may be any that keep to these rules, and one draw needn't show every extreme that they name: tile_mask is symmetric with ones on its diagonal; the share of nonzero tiles differs from tile row to tile row. `hamiltonian`: H is symmetric and H + I is positive definite.
All inputs are finite; a program needn't handle non-finite values.
Results may differ from the reference program's by a relative error of at most 0.0003.
Values sent between devices are 32-bit elements; how exact they have to be, the bound alone decides.
A program may use at most 64 MiB of HBM per device.

```python
import jax
import jax.numpy as jnp
from jax import lax

M = 16
K = 32
TILE = 256
ITERS = 3
N = 512
N_ROW = 8
N_COL = 4


def draw_hamiltonian(key, part):
    key = jax.random.fold_in(key, 11)
    total = M * N_ROW * N_COL
    first, second = jax.random.split(key)
    raw = jax.random.normal(first, (total, total), jnp.float32)
    sym = (raw + raw.T) * (0.25 / jnp.sqrt(jnp.float32(total)))
    energies = jax.random.uniform(second, (total,), jnp.float32, 0.0, 2.0)
    sym = sym + jnp.diag(energies)
    return sym.reshape(total, N_ROW, N_COL, M).transpose(0, 2, 1, 3).reshape(total, total)


def draw_tile_mask(key, part):
    key = jax.random.fold_in(key, 23)
    count = M * N_ROW * N_COL // TILE
    first, second = jax.random.split(key)
    weights = jax.random.randint(first, (count,), 1, 4)
    raw = jax.random.randint(second, (count, count), 0, 8)
    rows = jnp.arange(count)[:, None]
    cols = jnp.arange(count)[None, :]
    sym = jnp.where(rows <= cols, raw, raw.T)
    limit = weights[:, None] + weights[None, :]
    return jnp.where((sym < limit) | (rows == cols), 1, 0).astype(jnp.int32)


def shard_levels(rng, extent, cuts, low, top_value):
    def one(dim, shards_of):
        heights = jax.random.uniform(jax.random.fold_in(jax.random.fold_in(rng, 6), dim), (shards_of,), jnp.float32, low / len(cuts), top_value / len(cuts))
        return jnp.repeat(jnp.exp(heights), extent[dim] // shards_of).reshape((-1,) + (1,) * (len(extent) - dim - 1))

    level = one(*cuts[0])
    for cut in cuts[1:]:
        level = level * one(*cut)
    return level


def normal_values(stream_key, shape, spread, most, shards=(), kind=jnp.bfloat16):
    array = spread * jax.random.normal(stream_key, shape, jnp.float32)
    if shards:
        array = array * shard_levels(stream_key, shape, shards, -0.22, 0.18)
    return jnp.clip(array, -most, most).astype(kind)


def setup_inputs(seed: int = 0) -> dict:
    seeds = jax.random.split(jax.random.key(seed), 4)
    return {
        "hamiltonian": draw_hamiltonian(jax.random.fold_in(seeds[3], 71), 0),
        "tile_mask": draw_tile_mask(jax.random.fold_in(seeds[3], 71), 0),
        "start_block": normal_values(seeds[2], (N, K), 1.0, 6.0, ((0, 32),), jnp.float32),
    }


HIGH = lax.Precision.HIGHEST

def small_dot(left, right):
    return jnp.dot(left, right, precision=HIGH)

def inner(left, right):
    return lax.dot_general(left, right, (((0,), (0,)), ((), ())), precision=HIGH)

def cho_apply(lower, right):
    first = lax.linalg.triangular_solve(lower, right, left_side=True, lower=True)
    return lax.linalg.triangular_solve(lower, first, left_side=True, lower=True, transpose_a=True)

def ritz_step(basis, basis_image, gram, proj_raw, width):
    proj = 0.5 * (proj_raw + proj_raw.T)
    shifted = proj + 2.0 * gram
    solved = cho_apply(jnp.linalg.cholesky(shifted), gram[:, :width])
    normal_form = small_dot(solved.T, small_dot(gram, solved))
    normal_form = 0.5 * (normal_form + normal_form.T)
    factor = jnp.linalg.cholesky(normal_form)
    coeffs = lax.linalg.triangular_solve(factor, solved, left_side=False, lower=True, transpose_a=True)
    states = small_dot(basis, coeffs)
    image = small_dot(basis_image, coeffs)
    along = small_dot(basis[:, width:], coeffs[width:])
    along_image = small_dot(basis_image[:, width:], coeffs[width:])
    ritz = small_dot(coeffs.T, small_dot(proj, coeffs))
    return (states, image, along, along_image, ritz)

def reference(hamiltonian, tile_mask, start_block):
    total = hamiltonian.shape[0]
    width = start_block.shape[1]
    stored = jnp.arange(total)
    column = stored // (M * N_ROW)
    rest = stored % (M * N_ROW)
    vector_index = (rest // M * N_COL + column) * M + rest % M
    tile_column = vector_index // TILE
    bands = hamiltonian.reshape(total // TILE, TILE, total)

    def operate(vectors):
        reordered = vectors.reshape(N_ROW, N_COL, M, width).transpose(1, 0, 2, 3).reshape(total, width)

        def one_band(pair):
            band, mask_row = pair
            weights = mask_row[tile_column].astype(jnp.float32)
            return jnp.dot(band * weights[None, :], reordered, precision=HIGH)
        return lax.map(one_band, (bands, tile_mask)).reshape(total, width)
    states = start_block
    image = operate(states)
    gram = inner(states, states)
    theta = cho_apply(jnp.linalg.cholesky(gram), inner(states, image))
    resid = image - small_dot(states, theta)
    along = None
    along_image = None
    ritz = theta
    for step in range(ITERS):
        resid_image = operate(resid)
        if along is None:
            basis = jnp.concatenate([states, resid], axis=1)
            basis_image = jnp.concatenate([image, resid_image], axis=1)
        else:
            basis = jnp.concatenate([states, resid, along], axis=1)
            basis_image = jnp.concatenate([image, resid_image, along_image], axis=1)
        gram = inner(basis, basis)
        proj_raw = inner(basis, basis_image)
        states, image, along, along_image, ritz = ritz_step(basis, basis_image, gram, proj_raw, width)
        if step + 1 < ITERS:
            resid = image - small_dot(states, ritz)
    scale = jnp.sqrt(jnp.float32(total))
    return (states * scale, ritz)
```

```python
import functools

import jax
import jax.numpy as jnp
from jax import lax
from jax.experimental import pallas as pl
from jax.experimental.pallas import tpu as pltpu
from jax.sharding import PartitionSpec as P

TILE = 256
ITERS = 3
LANES = 128
SUB = 8
LOCAL_BYTES = 4 * 2**20

HIGH = lax.Precision.HIGHEST


def dot_nn(left, right):
    return lax.dot_general(
        left, right, (((1,), (0,)), ((), ())), precision=HIGH, preferred_element_type=jnp.float32
    )


def dot_nt(left, right):
    return lax.dot_general(
        left, right, (((1,), (1,)), ((), ())), precision=HIGH, preferred_element_type=jnp.float32
    )


def lane_splat(tile, lane):
    return jnp.broadcast_to(tile[:, lane : lane + 1], (SUB, LANES))


def row_splat(tile, row):
    return jnp.broadcast_to(tile[row : row + 1, :], (SUB, LANES))


def assemble(rows):
    sub = lax.broadcasted_iota(jnp.int32, (SUB, LANES), 0)
    tile = rows[0]
    for i in range(1, SUB):
        tile = jnp.where(sub == i, rows[i], tile)
    return tile


def eliminate(tiles, first_lane, factor):
    tiles = list(tiles)
    count = len(tiles)
    for p in range(count):
        base = first_lane + SUB * p
        others = range(p + 1, count) if factor else [t for t in range(count) if t != p]
        own = [lane_splat(tiles[p], base + k) for k in range(SUB)]
        block = {(i, k): row_splat(own[k], i) for k in range(SUB) for i in range(k, SUB)}
        rows = [row_splat(tiles[p], i) for i in range(SUB)]
        scaled = {}
        diag = []
        for k in range(SUB):
            if factor:
                root = lax.rsqrt(block[k, k])
                diag.append(root)
                inverse = root * root
            else:
                inverse = 1.0 / block[k, k]
                diag.append(inverse)
            for i in range(k + 1, SUB):
                scaled[i, k] = block[i, k] * inverse
            for i in range(k + 1, SUB):
                for q in range(k + 1, i + 1):
                    block[i, q] = block[i, q] - scaled[i, k] * block[q, k]
                rows[i] = rows[i] - scaled[i, k] * rows[k]
        rows = [rows[k] * diag[k] for k in range(SUB)]
        if factor:
            finished = assemble(rows)
            if p + 1 == count:
                tiles[p] = finished
                break
            rows = [rows[k] * diag[k] for k in range(SUB)]
        for k in range(SUB - 1, 0, -1):
            for i in range(k):
                rows[i] = rows[i] - scaled[k, i] * rows[k]
        for t in others:
            tile = tiles[t]
            for k in range(SUB):
                tile = tile - lane_splat(tiles[t], base + k) * rows[k]
            tiles[t] = tile
        tiles[p] = finished if factor else assemble(rows)
    return jnp.concatenate(tiles, axis=0)


def split_tiles(matrix):
    return [matrix[SUB * t : SUB * (t + 1)] for t in range(matrix.shape[0] // SUB)]


def solve_spd(matrix, width):
    return eliminate(split_tiles(matrix), width, False)[:, :width]


def pad_rows(pieces):
    rows = sum(piece.shape[0] for piece in pieces)
    if rows < LANES:
        pieces = pieces + [jnp.zeros((LANES - rows, pieces[0].shape[1]), jnp.float32)]
    return jnp.concatenate(pieces, axis=0)


def local_kernel(
    sizes, mask_ref, blocks_ref, start_ref, states_ref, ritz_ref, matrix, block, final
):
    row_count, col_count, piece, width = sizes
    local_rows = piece * col_count
    local_cols = piece * row_count
    total = piece * row_count * col_count
    stored = lax.broadcasted_iota(jnp.int32, (piece, local_cols), 1)
    for q in range(row_count):
        for c in range(col_count):
            tile_row = (q * col_count + c) * piece // TILE
            for d in range(col_count):
                tile_column = ((stored // piece * col_count + d) * piece + stored % piece) // TILE
                weights = jnp.zeros((piece, local_cols), jnp.float32)
                for t in range(total // TILE):
                    value = mask_ref[tile_row, t].astype(jnp.float32)
                    weights = jnp.where(tile_column == t, value, weights)
                first = (q * col_count + d) * local_rows + c * piece
                matrix[
                    c * local_cols + q * piece : c * local_cols + (q + 1) * piece,
                    d * local_cols : (d + 1) * local_cols,
                ] = blocks_ref[first : first + piece, :] * weights
            block[c * local_cols + q * piece : c * local_cols + (q + 1) * piece, :] = start_ref[
                (q * col_count + c) * piece : (q * col_count + c + 1) * piece, :
            ]
    states = block[...].T
    image = dot_nn(states, matrix[...])
    small = dot_nt(states, pad_rows([image, states]))
    theta = solve_spd(small, width)
    resid = image - dot_nn(theta.T, states)
    along = None
    for step in range(ITERS):
        resid_image = dot_nn(resid, matrix[...])
        if along is None:
            basis = jnp.concatenate([states, resid], axis=0)
            basis_image = jnp.concatenate([image, resid_image], axis=0)
        else:
            basis = jnp.concatenate([states, resid, along], axis=0)
            basis_image = jnp.concatenate([image, resid_image, along_image], axis=0)
        small = dot_nt(basis, pad_rows([states, basis_image + 2.0 * basis]))
        solved = solve_spd(small, width)
        both = jnp.concatenate([basis, basis_image], axis=1)
        tail = dot_nn(solved[width:].T, both[width:])
        whole = dot_nn(solved.T, both)
        zeros = jnp.zeros((width, total), jnp.float32)
        normal = dot_nt(whole[:, :total], pad_rows([zeros, whole[:, :total]]))
        lane = lax.broadcasted_iota(jnp.int32, (width, LANES), 1)
        sub = lax.broadcasted_iota(jnp.int32, (width, LANES), 0)
        normal = jnp.where(lane == sub, 1.0, normal)
        inverse = eliminate(split_tiles(normal), width, True)[:, :width]
        whole = dot_nn(inverse, whole)
        states, image = whole[:, :total], whole[:, total:]
        ritz = dot_nt(states, image)
        if step + 1 < ITERS:
            resid = image - dot_nn(ritz.T, states)
            tail = dot_nn(inverse, tail)
            along, along_image = tail[:, :total], tail[:, total:]
    ritz_ref[...] = 0.5 * (ritz + ritz.T)
    final[...] = (states * jnp.sqrt(jnp.float32(total))).T
    mine = lax.axis_index("col") * local_cols + lax.axis_index("row") * piece
    states_ref[...] = final[pl.ds(pl.multiple_of(mine, SUB), piece), :]


def local_body(hamiltonian, tile_mask, start_block):
    row_count = lax.axis_size("row")
    col_count = lax.axis_size("col")
    piece, width = start_block.shape
    total = piece * row_count * col_count
    blocks = lax.all_gather(hamiltonian, ("row", "col"), axis=0, tiled=True)
    start = lax.all_gather(start_block, ("row", "col"), axis=0, tiled=True)
    vmem = pl.BlockSpec(memory_space=pltpu.VMEM)
    return pl.pallas_call(
        functools.partial(local_kernel, (row_count, col_count, piece, width)),
        out_shape=(
            jax.ShapeDtypeStruct((piece, width), jnp.float32),
            jax.ShapeDtypeStruct((width, width), jnp.float32),
        ),
        in_specs=[pl.BlockSpec(memory_space=pltpu.SMEM), vmem, vmem],
        out_specs=(vmem, vmem),
        scratch_shapes=[
            pltpu.VMEM((total, total), jnp.float32),
            pltpu.VMEM((total, width), jnp.float32),
            pltpu.VMEM((total, width), jnp.float32),
        ],
        compiler_params=pltpu.CompilerParams(vmem_limit_bytes=32 * 2**20),
    )(tile_mask, blocks, start)


def small_dot(left, right):
    return jnp.dot(left, right, precision=HIGH)


def inner(left, right):
    return lax.dot_general(left, right, (((0,), (0,)), ((), ())), precision=HIGH)


def cho_apply(lower, right):
    first = lax.linalg.triangular_solve(lower, right, left_side=True, lower=True)
    return lax.linalg.triangular_solve(lower, first, left_side=True, lower=True, transpose_a=True)


def gram_sum(first, second):
    return lax.psum((first, second), ("row", "col"))


def ritz_step(basis, basis_image, gram, proj_raw, width):
    proj = 0.5 * (proj_raw + proj_raw.T)
    shifted = proj + 2.0 * gram
    solved = cho_apply(jnp.linalg.cholesky(shifted), gram[:, :width])
    normal_form = small_dot(solved.T, small_dot(gram, solved))
    normal_form = 0.5 * (normal_form + normal_form.T)
    factor = jnp.linalg.cholesky(normal_form)
    coeffs = lax.linalg.triangular_solve(
        factor, solved, left_side=False, lower=True, transpose_a=True
    )
    states = small_dot(basis, coeffs)
    image = small_dot(basis_image, coeffs)
    along = small_dot(basis[:, width:], coeffs[width:])
    along_image = small_dot(basis_image[:, width:], coeffs[width:])
    ritz = small_dot(coeffs.T, small_dot(proj, coeffs))
    return (states, image, along, along_image, ritz)


def body(hamiltonian, tile_mask, start_block):
    row_index = lax.axis_index("row")
    col_index = lax.axis_index("col")
    row_count = lax.axis_size("row")
    col_count = lax.axis_size("col")
    local_rows, local_cols = hamiltonian.shape
    piece = start_block.shape[0]
    width = start_block.shape[1]
    tile_row = (row_index * local_rows + jnp.arange(local_rows)) // TILE
    column = jnp.arange(local_cols)
    vector_index = (column // piece * col_count + col_index) * piece + column % piece
    tile_column = vector_index // TILE
    local_mask = jnp.take(jnp.take(tile_mask, tile_row, axis=0), tile_column, axis=1)
    masked = hamiltonian * local_mask.astype(jnp.float32)

    def operate(vectors):
        gathered = lax.all_gather(vectors, "row", axis=0, tiled=True)
        return lax.psum_scatter(
            jnp.dot(masked, gathered, precision=HIGH), "col", scatter_dimension=0, tiled=True
        )

    states = start_block
    image = operate(states)
    gram, product = gram_sum(inner(states, states), inner(states, image))
    theta = cho_apply(jnp.linalg.cholesky(gram), product)
    resid = image - small_dot(states, theta)
    along = None
    along_image = None
    ritz = theta
    for step in range(ITERS):
        resid_image = operate(resid)
        if along is None:
            basis = jnp.concatenate([states, resid], axis=1)
            basis_image = jnp.concatenate([image, resid_image], axis=1)
        else:
            basis = jnp.concatenate([states, resid, along], axis=1)
            basis_image = jnp.concatenate([image, resid_image, along_image], axis=1)
        gram, proj_raw = gram_sum(inner(basis, basis), inner(basis, basis_image))
        states, image, along, along_image, ritz = ritz_step(
            basis, basis_image, gram, proj_raw, width
        )
        if step + 1 < ITERS:
            resid = image - small_dot(states, ritz)
    total = piece * row_count * col_count
    scale = jnp.sqrt(jnp.float32(total))
    return (states * scale, ritz)


def solution(mesh):
    row_count, col_count = mesh.shape["row"], mesh.shape["col"]

    def shard(hamiltonian, tile_mask, start_block):
        piece = start_block.shape[0]
        size = (piece * row_count * col_count) ** 2 * 4
        whole = piece % SUB == 0 and piece * row_count % LANES == 0 and TILE % piece == 0
        run = local_body if whole and size <= LOCAL_BYTES else body
        return run(hamiltonian, tile_mask, start_block)

    placed = (P("row", "col"), P(), P(("row", "col"), None))
    return jax.shard_map(
        shard, mesh=mesh, in_specs=placed, out_specs=(P(("row", "col"), None), P()), check_vma=False
    )
```

```python
import functools

import jax
import jax.numpy as jnp
from jax import lax
from jax.experimental import pallas as pl
from jax.experimental.pallas import tpu as pltpu
from jax.sharding import PartitionSpec as P

TILE = 256
ITERS = 3
LANES = 128
SUB = 8
LOCAL_BYTES = 4 * 2**20

HIGH = lax.Precision.HIGHEST
MESH = pl.DeviceIdType.MESH


def flip(index, bit):
    return index + bit * (1 - 2 * ((index // bit) % 2))


def flip_all(index, bits):
    bit = 1
    while bit <= bits:
        if bits & bit:
            index = flip(index, bit)
        bit *= 2
    return index


def gather_kernel(
    row_count, col_count, matrix_ref, start_ref, out_ref, packed, local_sem, send_sem, recv_sem
):
    row, col = lax.axis_index("row"), lax.axis_index("col")
    rows = matrix_ref.shape[0]
    piece, width = start_ref.shape
    bits = [1 << i for i in range(row_count.bit_length() - 1)][::-1]
    orders = [bits, bits[:-1][::-1] + bits[-1:]]
    packed[0:rows, :] = matrix_ref[...]
    packed[rows:, :] = jnp.zeros((SUB, LANES), jnp.float32)
    for part in range(piece // SUB):
        packed[rows:, part * width : (part + 1) * width] = start_ref[
            part * SUB : (part + 1) * SUB, :
        ]

    barrier = pltpu.get_barrier_semaphore()
    for offset in range(1, col_count):
        pl.semaphore_signal(
            barrier, inc=1, device_id=(row, (col + offset) % col_count), device_id_type=MESH
        )
    for bit in bits:
        pl.semaphore_signal(barrier, inc=1, device_id=(flip(row, bit), col), device_id_type=MESH)
    pl.semaphore_wait(barrier, col_count - 1 + len(bits))

    def place(offset, member):
        source_col = (col + col_count - offset) % col_count
        return out_ref.at[flip_all(row, member) * col_count + source_col]

    def own_place():
        return out_ref.at[row * col_count + col]

    def copy(source, place_there, offset, member, device):
        return pltpu.make_async_remote_copy(
            src_ref=source,
            dst_ref=place_there,
            send_sem=send_sem.at[offset, member],
            recv_sem=recv_sem.at[offset, member],
            device_id=device,
            device_id_type=MESH,
        )

    sent = []
    for offset in range(1, col_count):
        away = copy(packed, own_place(), offset, 0, (row, (col + offset) % col_count))
        away.start()
        sent.append(away)
    keep = pltpu.make_async_copy(packed, own_place(), local_sem)
    arrivals = [(offset, member) for member in range(row_count) for offset in range(col_count)]

    def hops(item):
        offset, member = item
        return (member % 2, bin(member).count("1") + (offset > 0), offset)

    for offset, member in sorted(arrivals, key=hops):
        first = offset == 0 and member == 0
        source = packed if first else place(offset, member)
        if not first:
            copy(source, source, offset, member, (row, (col + 1) % col_count)).wait_recv()
        order = orders[offset % 2]
        done = [i for i, bit in enumerate(order) if member & bit]
        for bit in order[(done[-1] + 1 if done else 0) :]:
            onward = copy(
                source, place(offset, member), offset, member | bit, (flip(row, bit), col)
            )
            onward.start()
            sent.append(onward)
        if first:
            keep.start()
    for onward in sent:
        onward.wait_send()
    keep.wait()


def gather_blocks(hamiltonian, start_block):
    row_count, col_count = lax.axis_size("row"), lax.axis_size("col")
    vmem = pl.BlockSpec(memory_space=pltpu.VMEM)
    shape = (hamiltonian.shape[0] + SUB, LANES)
    sems = pltpu.SemaphoreType.DMA((col_count, row_count))
    return pl.pallas_call(
        functools.partial(gather_kernel, row_count, col_count),
        out_shape=jax.ShapeDtypeStruct((row_count * col_count, *shape), jnp.float32),
        in_specs=[vmem, vmem],
        out_specs=pl.BlockSpec(memory_space=pl.ANY),
        scratch_shapes=[
            pltpu.VMEM(shape, jnp.float32),
            pltpu.SemaphoreType.DMA,
            sems,
            sems,
        ],
        compiler_params=pltpu.CompilerParams(collective_id=0, has_side_effects=True),
    )(hamiltonian, start_block)


def dot_nn(left, right):
    return lax.dot_general(
        left, right, (((1,), (0,)), ((), ())), precision=HIGH, preferred_element_type=jnp.float32
    )


def dot_nt(left, right):
    return lax.dot_general(
        left, right, (((1,), (1,)), ((), ())), precision=HIGH, preferred_element_type=jnp.float32
    )


def lane_splat(tile, lane):
    return jnp.broadcast_to(tile[:, lane : lane + 1], (SUB, LANES))


def row_splat(tile, row):
    return jnp.broadcast_to(tile[row : row + 1, :], (SUB, LANES))


def assemble(rows):
    sub = lax.broadcasted_iota(jnp.int32, (SUB, LANES), 0)
    tile = rows[0]
    for i in range(1, SUB):
        tile = jnp.where(sub == i, rows[i], tile)
    return tile


def eliminate(tiles, first_lane, factor):
    tiles = list(tiles)
    count = len(tiles)
    for p in range(count):
        base = first_lane + SUB * p
        others = range(p + 1, count) if factor else [t for t in range(count) if t != p]
        own = [lane_splat(tiles[p], base + k) for k in range(SUB)]
        block = {(i, k): row_splat(own[k], i) for k in range(SUB) for i in range(k, SUB)}
        rows = [row_splat(tiles[p], i) for i in range(SUB)]
        scaled = {}
        diag = []
        for k in range(SUB):
            if factor:
                root = lax.rsqrt(block[k, k])
                diag.append(root)
                inverse = root * root
            else:
                inverse = 1.0 / block[k, k]
                diag.append(inverse)
            for i in range(k + 1, SUB):
                scaled[i, k] = block[i, k] * inverse
            for i in range(k + 1, SUB):
                for q in range(k + 1, i + 1):
                    block[i, q] = block[i, q] - scaled[i, k] * block[q, k]
                rows[i] = rows[i] - scaled[i, k] * rows[k]
        rows = [rows[k] * diag[k] for k in range(SUB)]
        if factor:
            finished = assemble(rows)
            if p + 1 == count:
                tiles[p] = finished
                break
            rows = [rows[k] * diag[k] for k in range(SUB)]
        for k in range(SUB - 1, 0, -1):
            for i in range(k):
                rows[i] = rows[i] - scaled[k, i] * rows[k]
        for t in others:
            tile = tiles[t]
            for k in range(SUB):
                tile = tile - lane_splat(tiles[t], base + k) * rows[k]
            tiles[t] = tile
        tiles[p] = finished if factor else assemble(rows)
    return jnp.concatenate(tiles, axis=0)


def split_tiles(matrix):
    return [matrix[SUB * t : SUB * (t + 1)] for t in range(matrix.shape[0] // SUB)]


def solve_spd(matrix, width):
    return eliminate(split_tiles(matrix), width, False)[:, :width]


def pad_rows(pieces):
    rows = sum(piece.shape[0] for piece in pieces)
    if rows < LANES:
        pieces = pieces + [jnp.zeros((LANES - rows, pieces[0].shape[1]), jnp.float32)]
    return jnp.concatenate(pieces, axis=0)


def local_kernel(
    sizes, mask_ref, blocks_ref, states_ref, ritz_ref, matrix, block, final
):
    row_count, col_count, piece, width = sizes
    local_rows = piece * col_count
    local_cols = piece * row_count
    total = piece * row_count * col_count
    stored = lax.broadcasted_iota(jnp.int32, (piece, local_cols), 1)
    for q in range(row_count):
        for c in range(col_count):
            tile_row = (q * col_count + c) * piece // TILE
            for d in range(col_count):
                tile_column = ((stored // piece * col_count + d) * piece + stored % piece) // TILE
                weights = jnp.zeros((piece, local_cols), jnp.float32)
                for t in range(total // TILE):
                    value = mask_ref[tile_row, t].astype(jnp.float32)
                    weights = jnp.where(tile_column == t, value, weights)
                matrix[
                    c * local_cols + q * piece : c * local_cols + (q + 1) * piece,
                    d * local_cols : (d + 1) * local_cols,
                ] = blocks_ref[q * col_count + d, c * piece : (c + 1) * piece, :] * weights
            for part in range(piece // SUB):
                first = c * local_cols + q * piece + part * SUB
                block[first : first + SUB, :] = blocks_ref[
                    q * col_count + c, local_rows:, part * width : (part + 1) * width
                ]
    states = block[...].T
    image = dot_nn(states, matrix[...])
    small = dot_nt(states, pad_rows([image, states]))
    theta = solve_spd(small, width)
    resid = image - dot_nn(theta.T, states)
    along = None
    for step in range(ITERS):
        resid_image = dot_nn(resid, matrix[...])
        if along is None:
            basis = jnp.concatenate([states, resid], axis=0)
            basis_image = jnp.concatenate([image, resid_image], axis=0)
        else:
            basis = jnp.concatenate([states, resid, along], axis=0)
            basis_image = jnp.concatenate([image, resid_image, along_image], axis=0)
        small = dot_nt(basis, pad_rows([states, basis_image + 2.0 * basis]))
        solved = solve_spd(small, width)
        both = jnp.concatenate([basis, basis_image], axis=1)
        tail = dot_nn(solved[width:].T, both[width:])
        whole = dot_nn(solved.T, both)
        zeros = jnp.zeros((width, total), jnp.float32)
        normal = dot_nt(whole[:, :total], pad_rows([zeros, whole[:, :total]]))
        lane = lax.broadcasted_iota(jnp.int32, (width, LANES), 1)
        sub = lax.broadcasted_iota(jnp.int32, (width, LANES), 0)
        normal = jnp.where(lane == sub, 1.0, normal)
        inverse = eliminate(split_tiles(normal), width, True)[:, :width]
        whole = dot_nn(inverse, whole)
        states, image = whole[:, :total], whole[:, total:]
        ritz = dot_nt(states, image)
        if step + 1 < ITERS:
            resid = image - dot_nn(ritz.T, states)
            tail = dot_nn(inverse, tail)
            along, along_image = tail[:, :total], tail[:, total:]
    ritz_ref[...] = 0.5 * (ritz + ritz.T)
    final[...] = (states * jnp.sqrt(jnp.float32(total))).T
    mine = lax.axis_index("col") * local_cols + lax.axis_index("row") * piece
    states_ref[...] = final[pl.ds(pl.multiple_of(mine, SUB), piece), :]


def local_body(hamiltonian, tile_mask, start_block):
    row_count = lax.axis_size("row")
    col_count = lax.axis_size("col")
    piece, width = start_block.shape
    total = piece * row_count * col_count
    blocks = gather_blocks(hamiltonian, start_block)
    vmem = pl.BlockSpec(memory_space=pltpu.VMEM)
    return pl.pallas_call(
        functools.partial(local_kernel, (row_count, col_count, piece, width)),
        out_shape=(
            jax.ShapeDtypeStruct((piece, width), jnp.float32),
            jax.ShapeDtypeStruct((width, width), jnp.float32),
        ),
        in_specs=[pl.BlockSpec(memory_space=pltpu.SMEM), vmem],
        out_specs=(vmem, vmem),
        scratch_shapes=[
            pltpu.VMEM((total, total), jnp.float32),
            pltpu.VMEM((total, width), jnp.float32),
            pltpu.VMEM((total, width), jnp.float32),
        ],
        compiler_params=pltpu.CompilerParams(vmem_limit_bytes=32 * 2**20),
    )(tile_mask, blocks)


def small_dot(left, right):
    return jnp.dot(left, right, precision=HIGH)


def inner(left, right):
    return lax.dot_general(left, right, (((0,), (0,)), ((), ())), precision=HIGH)


def cho_apply(lower, right):
    first = lax.linalg.triangular_solve(lower, right, left_side=True, lower=True)
    return lax.linalg.triangular_solve(lower, first, left_side=True, lower=True, transpose_a=True)


def gram_sum(first, second):
    return lax.psum((first, second), ("row", "col"))


def ritz_step(basis, basis_image, gram, proj_raw, width):
    proj = 0.5 * (proj_raw + proj_raw.T)
    shifted = proj + 2.0 * gram
    solved = cho_apply(jnp.linalg.cholesky(shifted), gram[:, :width])
    normal_form = small_dot(solved.T, small_dot(gram, solved))
    normal_form = 0.5 * (normal_form + normal_form.T)
    factor = jnp.linalg.cholesky(normal_form)
    coeffs = lax.linalg.triangular_solve(
        factor, solved, left_side=False, lower=True, transpose_a=True
    )
    states = small_dot(basis, coeffs)
    image = small_dot(basis_image, coeffs)
    along = small_dot(basis[:, width:], coeffs[width:])
    along_image = small_dot(basis_image[:, width:], coeffs[width:])
    ritz = small_dot(coeffs.T, small_dot(proj, coeffs))
    return (states, image, along, along_image, ritz)


def body(hamiltonian, tile_mask, start_block):
    row_index = lax.axis_index("row")
    col_index = lax.axis_index("col")
    row_count = lax.axis_size("row")
    col_count = lax.axis_size("col")
    local_rows, local_cols = hamiltonian.shape
    piece = start_block.shape[0]
    width = start_block.shape[1]
    tile_row = (row_index * local_rows + jnp.arange(local_rows)) // TILE
    column = jnp.arange(local_cols)
    vector_index = (column // piece * col_count + col_index) * piece + column % piece
    tile_column = vector_index // TILE
    local_mask = jnp.take(jnp.take(tile_mask, tile_row, axis=0), tile_column, axis=1)
    masked = hamiltonian * local_mask.astype(jnp.float32)

    def operate(vectors):
        gathered = lax.all_gather(vectors, "row", axis=0, tiled=True)
        return lax.psum_scatter(
            jnp.dot(masked, gathered, precision=HIGH), "col", scatter_dimension=0, tiled=True
        )

    states = start_block
    image = operate(states)
    gram, product = gram_sum(inner(states, states), inner(states, image))
    theta = cho_apply(jnp.linalg.cholesky(gram), product)
    resid = image - small_dot(states, theta)
    along = None
    along_image = None
    ritz = theta
    for step in range(ITERS):
        resid_image = operate(resid)
        if along is None:
            basis = jnp.concatenate([states, resid], axis=1)
            basis_image = jnp.concatenate([image, resid_image], axis=1)
        else:
            basis = jnp.concatenate([states, resid, along], axis=1)
            basis_image = jnp.concatenate([image, resid_image, along_image], axis=1)
        gram, proj_raw = gram_sum(inner(basis, basis), inner(basis, basis_image))
        states, image, along, along_image, ritz = ritz_step(
            basis, basis_image, gram, proj_raw, width
        )
        if step + 1 < ITERS:
            resid = image - small_dot(states, ritz)
    total = piece * row_count * col_count
    scale = jnp.sqrt(jnp.float32(total))
    return (states * scale, ritz)


def solution(mesh):
    row_count, col_count = mesh.shape["row"], mesh.shape["col"]

    def shard(hamiltonian, tile_mask, start_block):
        piece = start_block.shape[0]
        size = (piece * row_count * col_count) ** 2 * 4
        whole = piece % SUB == 0 and piece * row_count == LANES and TILE % piece == 0
        whole = whole and start_block.shape[1] * (piece // SUB) <= LANES
        whole = whole and row_count & (row_count - 1) == 0 and row_count > 1 and col_count > 1
        run = local_body if whole and size <= LOCAL_BYTES else body
        return run(hamiltonian, tile_mask, start_block)

    placed = (P("row", "col"), P(), P(("row", "col"), None))
    return jax.shard_map(
        shard, mesh=mesh, in_specs=placed, out_specs=(P(("row", "col"), None), P()), check_vma=False
    )
```

```python
import functools

import jax
import jax.numpy as jnp
from jax import lax
from jax.experimental import pallas as pl
from jax.experimental.pallas import tpu as pltpu
from jax.sharding import PartitionSpec as P

TILE = 256
ITERS = 3
LANES = 128
SUB = 8
LOCAL_BYTES = 4 * 2**20

HIGH = lax.Precision.HIGHEST
MESH = pl.DeviceIdType.MESH


def flip(index, bit):
    return index + bit * (1 - 2 * ((index // bit) % 2))


def flip_all(index, bits):
    bit = 1
    while bit <= bits:
        if bits & bit:
            index = flip(index, bit)
        bit *= 2
    return index


def gather_kernel(
    row_count, col_count, matrix_ref, start_ref, out_ref, packed, local_sem, send_sem, recv_sem
):
    row, col = lax.axis_index("row"), lax.axis_index("col")
    rows = matrix_ref.shape[0]
    piece, width = start_ref.shape
    bits = [1 << i for i in range(row_count.bit_length() - 1)][::-1]
    orders = [bits, bits[:-1][::-1] + bits[-1:]]
    packed[0:rows, :] = matrix_ref[...]
    packed[rows:, :] = jnp.zeros((SUB, LANES), jnp.float32)
    for part in range(piece // SUB):
        packed[rows:, part * width : (part + 1) * width] = start_ref[
            part * SUB : (part + 1) * SUB, :
        ]

    barrier = pltpu.get_barrier_semaphore()
    for offset in range(1, col_count):
        pl.semaphore_signal(
            barrier, inc=1, device_id=(row, (col + offset) % col_count), device_id_type=MESH
        )
    for bit in bits:
        pl.semaphore_signal(barrier, inc=1, device_id=(flip(row, bit), col), device_id_type=MESH)
    pl.semaphore_wait(barrier, col_count - 1 + len(bits))

    def place(offset, member):
        source_col = (col + col_count - offset) % col_count
        return out_ref.at[flip_all(row, member) * col_count + source_col]

    def own_place():
        return out_ref.at[row * col_count + col]

    def copy(source, place_there, offset, member, device):
        return pltpu.make_async_remote_copy(
            src_ref=source,
            dst_ref=place_there,
            send_sem=send_sem.at[offset, member],
            recv_sem=recv_sem.at[offset, member],
            device_id=device,
            device_id_type=MESH,
        )

    sent = []
    for offset in range(1, col_count):
        away = copy(packed, own_place(), offset, 0, (row, (col + offset) % col_count))
        away.start()
        sent.append(away)
    keep = pltpu.make_async_copy(packed, own_place(), local_sem)
    arrivals = [(offset, member) for member in range(row_count) for offset in range(col_count)]

    def hops(item):
        offset, member = item
        return (member % 2, bin(member).count("1") + (offset > 0), offset)

    for offset, member in sorted(arrivals, key=hops):
        first = offset == 0 and member == 0
        source = packed if first else place(offset, member)
        if not first:
            copy(source, source, offset, member, (row, (col + 1) % col_count)).wait_recv()
        order = orders[offset % 2]
        done = [i for i, bit in enumerate(order) if member & bit]
        for bit in order[(done[-1] + 1 if done else 0) :]:
            onward = copy(
                source, place(offset, member), offset, member | bit, (flip(row, bit), col)
            )
            onward.start()
            sent.append(onward)
        if first:
            keep.start()
    for onward in sent:
        onward.wait_send()
    keep.wait()


def gather_blocks(hamiltonian, start_block):
    row_count, col_count = lax.axis_size("row"), lax.axis_size("col")
    vmem = pl.BlockSpec(memory_space=pltpu.VMEM)
    shape = (hamiltonian.shape[0] + SUB, LANES)
    sems = pltpu.SemaphoreType.DMA((col_count, row_count))
    return pl.pallas_call(
        functools.partial(gather_kernel, row_count, col_count),
        out_shape=jax.ShapeDtypeStruct((row_count * col_count, *shape), jnp.float32),
        in_specs=[vmem, vmem],
        out_specs=vmem,
        scratch_shapes=[
            pltpu.VMEM(shape, jnp.float32),
            pltpu.SemaphoreType.DMA,
            sems,
            sems,
        ],
        compiler_params=pltpu.CompilerParams(collective_id=0, has_side_effects=True),
    )(hamiltonian, start_block)


def dot_nn(left, right):
    return lax.dot_general(
        left, right, (((1,), (0,)), ((), ())), precision=HIGH, preferred_element_type=jnp.float32
    )


def dot_nt(left, right):
    return lax.dot_general(
        left, right, (((1,), (1,)), ((), ())), precision=HIGH, preferred_element_type=jnp.float32
    )


def lane_splat(tile, lane):
    return jnp.broadcast_to(tile[:, lane : lane + 1], (SUB, LANES))


def row_splat(tile, row):
    return jnp.broadcast_to(tile[row : row + 1, :], (SUB, LANES))


def assemble(rows):
    sub = lax.broadcasted_iota(jnp.int32, (SUB, LANES), 0)
    tile = rows[0]
    for i in range(1, SUB):
        tile = jnp.where(sub == i, rows[i], tile)
    return tile


def eliminate(tiles, first_lane, factor):
    tiles = list(tiles)
    count = len(tiles)
    for p in range(count):
        base = first_lane + SUB * p
        others = range(p + 1, count) if factor else [t for t in range(count) if t != p]
        own = [lane_splat(tiles[p], base + k) for k in range(SUB)]
        block = {(i, k): row_splat(own[k], i) for k in range(SUB) for i in range(k, SUB)}
        rows = [row_splat(tiles[p], i) for i in range(SUB)]
        scaled = {}
        diag = []
        for k in range(SUB):
            if factor:
                root = lax.rsqrt(block[k, k])
                diag.append(root)
                inverse = root * root
            else:
                inverse = 1.0 / block[k, k]
                diag.append(inverse)
            for i in range(k + 1, SUB):
                scaled[i, k] = block[i, k] * inverse
            for i in range(k + 1, SUB):
                for q in range(k + 1, i + 1):
                    block[i, q] = block[i, q] - scaled[i, k] * block[q, k]
                rows[i] = rows[i] - scaled[i, k] * rows[k]
        rows = [rows[k] * diag[k] for k in range(SUB)]
        if factor:
            finished = assemble(rows)
            if p + 1 == count:
                tiles[p] = finished
                break
            rows = [rows[k] * diag[k] for k in range(SUB)]
        for k in range(SUB - 1, 0, -1):
            for i in range(k):
                rows[i] = rows[i] - scaled[k, i] * rows[k]
        for t in others:
            tile = tiles[t]
            for k in range(SUB):
                tile = tile - lane_splat(tiles[t], base + k) * rows[k]
            tiles[t] = tile
        tiles[p] = finished if factor else assemble(rows)
    return jnp.concatenate(tiles, axis=0)


def split_tiles(matrix):
    return [matrix[SUB * t : SUB * (t + 1)] for t in range(matrix.shape[0] // SUB)]


def solve_spd(matrix, width):
    return eliminate(split_tiles(matrix), width, False)[:, :width]


def pad_rows(pieces):
    rows = sum(piece.shape[0] for piece in pieces)
    if rows < LANES:
        pieces = pieces + [jnp.zeros((LANES - rows, pieces[0].shape[1]), jnp.float32)]
    return jnp.concatenate(pieces, axis=0)


def local_kernel(
    sizes, mask_ref, blocks_ref, states_ref, ritz_ref, matrix, block, final
):
    row_count, col_count, piece, width = sizes
    local_rows = piece * col_count
    local_cols = piece * row_count
    total = piece * row_count * col_count
    stored = lax.broadcasted_iota(jnp.int32, (piece, local_cols), 1)
    for q in range(row_count):
        for c in range(col_count):
            tile_row = (q * col_count + c) * piece // TILE
            for d in range(col_count):
                tile_column = ((stored // piece * col_count + d) * piece + stored % piece) // TILE
                weights = jnp.zeros((piece, local_cols), jnp.float32)
                for t in range(total // TILE):
                    value = mask_ref[tile_row, t].astype(jnp.float32)
                    weights = jnp.where(tile_column == t, value, weights)
                matrix[
                    c * local_cols + q * piece : c * local_cols + (q + 1) * piece,
                    d * local_cols : (d + 1) * local_cols,
                ] = blocks_ref[q * col_count + d, c * piece : (c + 1) * piece, :] * weights
            for part in range(piece // SUB):
                first = c * local_cols + q * piece + part * SUB
                block[first : first + SUB, :] = blocks_ref[
                    q * col_count + c, local_rows:, part * width : (part + 1) * width
                ]
    states = block[...].T
    image = dot_nn(states, matrix[...])
    small = dot_nt(states, pad_rows([image, states]))
    theta = solve_spd(small, width)
    resid = image - dot_nn(theta.T, states)
    along = None
    for step in range(ITERS):
        resid_image = dot_nn(resid, matrix[...])
        if along is None:
            basis = jnp.concatenate([states, resid], axis=0)
            basis_image = jnp.concatenate([image, resid_image], axis=0)
        else:
            basis = jnp.concatenate([states, resid, along], axis=0)
            basis_image = jnp.concatenate([image, resid_image, along_image], axis=0)
        small = dot_nt(basis, pad_rows([states, basis_image + 2.0 * basis]))
        solved = solve_spd(small, width)
        both = jnp.concatenate([basis, basis_image], axis=1)
        whole = dot_nn(solved.T, both)
        zeros = jnp.zeros((width, total), jnp.float32)
        normal = dot_nt(whole[:, :total], pad_rows([zeros, whole[:, :total]]))
        lane = lax.broadcasted_iota(jnp.int32, (width, LANES), 1)
        sub = lax.broadcasted_iota(jnp.int32, (width, LANES), 0)
        normal = jnp.where(lane == sub, 1.0, normal)
        inverse = eliminate(split_tiles(normal), width, True)[:, :width]
        whole = dot_nn(inverse, whole)
        states, image = whole[:, :total], whole[:, total:]
        ritz = dot_nt(states, image)
        if step + 1 < ITERS:
            resid = image - dot_nn(ritz.T, states)
            tail = dot_nn(inverse, dot_nn(solved[width:].T, both[width:]))
            along, along_image = tail[:, :total], tail[:, total:]
    ritz_ref[...] = 0.5 * (ritz + ritz.T)
    final[...] = (states * jnp.sqrt(jnp.float32(total))).T
    mine = lax.axis_index("col") * local_cols + lax.axis_index("row") * piece
    states_ref[...] = final[pl.ds(pl.multiple_of(mine, SUB), piece), :]


def local_body(hamiltonian, tile_mask, start_block):
    row_count = lax.axis_size("row")
    col_count = lax.axis_size("col")
    piece, width = start_block.shape
    total = piece * row_count * col_count
    blocks = gather_blocks(hamiltonian, start_block)
    vmem = pl.BlockSpec(memory_space=pltpu.VMEM)
    return pl.pallas_call(
        functools.partial(local_kernel, (row_count, col_count, piece, width)),
        out_shape=(
            jax.ShapeDtypeStruct((piece, width), jnp.float32),
            jax.ShapeDtypeStruct((width, width), jnp.float32),
        ),
        in_specs=[pl.BlockSpec(memory_space=pltpu.SMEM), vmem],
        out_specs=(vmem, vmem),
        scratch_shapes=[
            pltpu.VMEM((total, total), jnp.float32),
            pltpu.VMEM((total, width), jnp.float32),
            pltpu.VMEM((total, width), jnp.float32),
        ],
        compiler_params=pltpu.CompilerParams(vmem_limit_bytes=32 * 2**20),
    )(tile_mask, blocks)


def small_dot(left, right):
    return jnp.dot(left, right, precision=HIGH)


def inner(left, right):
    return lax.dot_general(left, right, (((0,), (0,)), ((), ())), precision=HIGH)


def cho_apply(lower, right):
    first = lax.linalg.triangular_solve(lower, right, left_side=True, lower=True)
    return lax.linalg.triangular_solve(lower, first, left_side=True, lower=True, transpose_a=True)


def gram_sum(first, second):
    return lax.psum((first, second), ("row", "col"))


def ritz_step(basis, basis_image, gram, proj_raw, width):
    proj = 0.5 * (proj_raw + proj_raw.T)
    shifted = proj + 2.0 * gram
    solved = cho_apply(jnp.linalg.cholesky(shifted), gram[:, :width])
    normal_form = small_dot(solved.T, small_dot(gram, solved))
    normal_form = 0.5 * (normal_form + normal_form.T)
    factor = jnp.linalg.cholesky(normal_form)
    coeffs = lax.linalg.triangular_solve(
        factor, solved, left_side=False, lower=True, transpose_a=True
    )
    states = small_dot(basis, coeffs)
    image = small_dot(basis_image, coeffs)
    along = small_dot(basis[:, width:], coeffs[width:])
    along_image = small_dot(basis_image[:, width:], coeffs[width:])
    ritz = small_dot(coeffs.T, small_dot(proj, coeffs))
    return (states, image, along, along_image, ritz)


def body(hamiltonian, tile_mask, start_block):
    row_index = lax.axis_index("row")
    col_index = lax.axis_index("col")
    row_count = lax.axis_size("row")
    col_count = lax.axis_size("col")
    local_rows, local_cols = hamiltonian.shape
    piece = start_block.shape[0]
    width = start_block.shape[1]
    tile_row = (row_index * local_rows + jnp.arange(local_rows)) // TILE
    column = jnp.arange(local_cols)
    vector_index = (column // piece * col_count + col_index) * piece + column % piece
    tile_column = vector_index // TILE
    local_mask = jnp.take(jnp.take(tile_mask, tile_row, axis=0), tile_column, axis=1)
    masked = hamiltonian * local_mask.astype(jnp.float32)

    def operate(vectors):
        gathered = lax.all_gather(vectors, "row", axis=0, tiled=True)
        return lax.psum_scatter(
            jnp.dot(masked, gathered, precision=HIGH), "col", scatter_dimension=0, tiled=True
        )

    states = start_block
    image = operate(states)
    gram, product = gram_sum(inner(states, states), inner(states, image))
    theta = cho_apply(jnp.linalg.cholesky(gram), product)
    resid = image - small_dot(states, theta)
    along = None
    along_image = None
    ritz = theta
    for step in range(ITERS):
        resid_image = operate(resid)
        if along is None:
            basis = jnp.concatenate([states, resid], axis=1)
            basis_image = jnp.concatenate([image, resid_image], axis=1)
        else:
            basis = jnp.concatenate([states, resid, along], axis=1)
            basis_image = jnp.concatenate([image, resid_image, along_image], axis=1)
        gram, proj_raw = gram_sum(inner(basis, basis), inner(basis, basis_image))
        states, image, along, along_image, ritz = ritz_step(
            basis, basis_image, gram, proj_raw, width
        )
        if step + 1 < ITERS:
            resid = image - small_dot(states, ritz)
    total = piece * row_count * col_count
    scale = jnp.sqrt(jnp.float32(total))
    return (states * scale, ritz)


def solution(mesh):
    row_count, col_count = mesh.shape["row"], mesh.shape["col"]

    def shard(hamiltonian, tile_mask, start_block):
        piece = start_block.shape[0]
        size = (piece * row_count * col_count) ** 2 * 4
        whole = piece % SUB == 0 and piece * row_count == LANES and TILE % piece == 0
        whole = whole and start_block.shape[1] * (piece // SUB) <= LANES
        whole = whole and row_count & (row_count - 1) == 0 and row_count > 1 and col_count > 1
        run = local_body if whole and size <= LOCAL_BYTES else body
        return run(hamiltonian, tile_mask, start_block)

    placed = (P("row", "col"), P(), P(("row", "col"), None))
    return jax.shard_map(
        shard, mesh=mesh, in_specs=placed, out_specs=(P(("row", "col"), None), P()), check_vma=False
    )
```
